32 devices in a mesh: rep: 2 (over y), exp: 16 (over z, x, core).
Axes of the slice: x: 2, y: 2, z: 4, core: 2. Of those that a mesh axis runs over, the one named last changes fastest.
Arguments:
- tokens: bfloat16 [4096, 2048], P(('rep', 'exp')), may hold values from -6 to 6
- out_grad: bfloat16 [4096, 2048], P(('rep', 'exp')), may hold values from -1.5 to 1.5
- route: int32 [4096, 4], P(('rep', 'exp')), may hold values from 0 to 15, as said below
- prob: bfloat16 [4096, 4], P(('rep', 'exp')), may hold values from 0.049804688 to 0.59765625
- w_gate: bfloat16 [16, 2048, 384], P('exp'), may hold values from -0.125 to 0.125
- w_up: bfloat16 [16, 2048, 384], P('exp'), may hold values from -0.125 to 0.125
- w_down: bfloat16 [16, 384, 2048], P('exp'), may hold values from -0.3125 to 0.3125
Outputs:
- grad_tokens: bfloat16 [4096, 2048], P(('rep', 'exp'))
- grad_prob: bfloat16 [4096, 4], P(('rep', 'exp'))
- grad_gate: bfloat16 [16, 2048, 384], P('exp', 'rep')
- grad_up: bfloat16 [16, 2048, 384], P('exp', 'rep')
- grad_down: bfloat16 [16, 384, 2048], P('exp', 'rep')
The draws below stay inside these ranges and needn't reach their ends.
Inputs may be any that keep to these rules, and one draw needn't show every extreme that they name: `route`: each row names 4 different experts. In each aligned block of 128 rows (the rows of one device) an expert is named by at most 64 rows; one expert, the same for all blocks, is named by exactly 64 rows of every block.
All inputs are finite; a program needn't handle non-finite values.
Results may differ from the reference program's by a relative error of at most 0.0059.
Values may be sent and summed in bfloat16 or wider, within the bound.
A program may use at most 128 MiB of HBM per device.

```python
import jax
import jax.numpy as jnp
from jax import lax

D = 2048
F = 384
K = 4
TOK_DEV = 128
E = 16
TOKENS = 4096
CAP = 64
N_REP = 2


def draw_route(key, part):
    blocks = TOKENS // TOK_DEV
    rates = jax.random.randint(jax.random.fold_in(key, 11), (E,), 1, 17)
    favored = jax.random.randint(jax.random.fold_in(key, 12), (), 0, E)
    block_keys = jax.random.split(jax.random.fold_in(key, 13), blocks)
    labels = jnp.arange(E, dtype=jnp.int32)

    def one_block(block_key):
        keys = jax.random.split(block_key, 3)
        forced = jax.random.permutation(keys[0], TOK_DEV) < CAP
        noise = jax.random.randint(keys[1], (TOK_DEV, E), 0, 65536)
        shuffle = jax.random.randint(keys[2], (TOK_DEV, K), 0, 65536)

        def advance(counts, inputs):
            force_here, row_noise = inputs
            score = row_noise * rates * E + labels
            score = jnp.where(counts >= CAP, -1 - labels, score)
            score = jnp.where(labels == favored, jnp.where(force_here, 2 ** 30, -4 * E), score)
            picked = lax.top_k(score, K)[1].astype(jnp.int32)
            counts = counts + jnp.sum((picked[:, None] == labels[None, :]).astype(jnp.int32), axis=0)
            return (counts, picked)
        final_counts, picked = lax.scan(advance, jnp.zeros((E,), jnp.int32), (forced, noise))
        arrange = jnp.argsort(shuffle, axis=1, stable=True)
        return jnp.take_along_axis(picked, arrange, axis=1)
    return jax.vmap(one_block)(block_keys).reshape(TOKENS, K).astype(jnp.int32)


def steps_of(rng, extent, cuts, smallest, largest):
    def one(position, blocks):
        steps = jax.random.uniform(jax.random.fold_in(jax.random.fold_in(rng, 6), position), (blocks,), jnp.float32, smallest / len(cuts), largest / len(cuts))
        return jnp.repeat(jnp.exp(steps), extent[position] // blocks).reshape((-1,) + (1,) * (len(extent) - position - 1))

    level = one(*cuts[0])
    for cut in cuts[1:]:
        level = level * one(*cut)
    return level


def scatter_about(own_key, extent, spread, bound, cuts=(), kind=jnp.bfloat16):
    result = jax.random.normal(own_key, extent, jnp.float32) * spread
    if len(cuts) > 0:
        result = steps_of(own_key, extent, cuts, -0.22, 0.18) * result
    return jnp.clip(result, min=-bound, max=bound).astype(kind)


def setup_inputs(seed: int = 0) -> dict:
    arg_keys = jax.random.split(jax.random.key(seed), 8)
    tokens = scatter_about(arg_keys[0], (TOKENS, D), 1.0, 6.0, ((0, 32),))
    out_grad = scatter_about(arg_keys[1], (TOKENS, D), 0.25, 1.5, ((0, 32),))
    route = draw_route(jax.random.fold_in(arg_keys[7], 71), 0)
    prob = jnp.clip(0.049804688 + 0.54785156 * jax.random.uniform(arg_keys[3], (TOKENS, K), jnp.float32) ** steps_of(arg_keys[3], (TOKENS, K), ((0, 32),), -0.2, 0.2), 0.049804688, 0.59765625).astype(jnp.bfloat16)
    w_gate = scatter_about(arg_keys[4], (E, D, F), D ** -0.5, 0.125, ((0, 16),))
    w_up = scatter_about(arg_keys[5], (E, D, F), D ** -0.5, 0.125, ((0, 16),))
    w_down = scatter_about(arg_keys[6], (E, F, D), F ** -0.5, 0.3125, ((0, 16),))
    return dict(tokens=tokens, out_grad=out_grad, route=route, prob=prob, w_gate=w_gate, w_up=w_up, w_down=w_down)


def expert_pass(input_rows, row_gradients, rows_prob, gate_weight, up_weight, down_weight):
    gate_preactivation = jnp.dot(input_rows, gate_weight, preferred_element_type=jnp.float32)
    up_preactivation = jnp.dot(input_rows, up_weight, preferred_element_type=jnp.float32)
    backward_rows = jnp.dot(row_gradients, down_weight.T, preferred_element_type=jnp.float32)
    sigma = jax.nn.sigmoid(gate_preactivation)
    active = gate_preactivation * sigma
    hidden = active * up_preactivation
    grad_weight = jnp.sum(backward_rows * hidden, axis=-1).astype(jnp.bfloat16)
    weight = rows_prob.astype(jnp.float32)[:, None]
    scaled_output = (weight * hidden).astype(jnp.bfloat16)
    d_back = weight * backward_rows
    gate_gradient = (d_back * up_preactivation * sigma * (1.0 + gate_preactivation * (1.0 - sigma))).astype(jnp.bfloat16)
    up_gradient = (d_back * active).astype(jnp.bfloat16)
    contrib = jnp.dot(gate_gradient, gate_weight.T, preferred_element_type=jnp.float32)
    contrib = (contrib + jnp.dot(up_gradient, up_weight.T, preferred_element_type=jnp.float32)).astype(jnp.bfloat16)
    return contrib, grad_weight, scaled_output, gate_gradient, up_gradient


def group_sums(left, right, groups):
    total = jnp.zeros((left.shape[1], right.shape[1]), jnp.float32)
    for group in range(N_REP):
        inside = (groups == group)[:, None]
        masked = jnp.where(inside, left, jnp.zeros((), left.dtype))
        part = jnp.dot(masked.T, right, preferred_element_type=jnp.float32).astype(jnp.bfloat16)
        total = total + lax.optimization_barrier(part).astype(jnp.float32)
    return total.astype(jnp.bfloat16)


def reference(tokens, out_grad, route, prob, w_gate, w_up, w_down):
    flat = route.reshape(-1).astype(jnp.int32)
    labels = jnp.arange(E, dtype=jnp.int32)
    counts = jnp.sum((flat[:, None] == labels[None, :]).astype(jnp.int32), axis=0)
    starts = (jnp.cumsum(counts) - counts).astype(jnp.int32)
    most = (TOKENS // TOK_DEV) * CAP
    order = jnp.concatenate([jnp.argsort(flat, stable=True).astype(jnp.int32), jnp.zeros((most,), jnp.int32)])
    prob_flat = prob.reshape(-1)
    group_rows = TOKENS // N_REP

    def visit(carry, inputs):
        grad_acc, prob_acc = carry
        expert, gate_weight, up_weight, down_weight = inputs
        picks = lax.dynamic_slice_in_dim(order, starts[expert], most)
        valid = jnp.arange(most, dtype=jnp.int32) < counts[expert]
        rows = (picks // K).astype(jnp.int32)
        groups = (rows // group_rows).astype(jnp.int32)
        input_rows = jnp.where(valid[:, None], tokens[rows], jnp.zeros((), tokens.dtype))
        row_gradients = jnp.where(valid[:, None], out_grad[rows], jnp.zeros((), out_grad.dtype))
        rows_prob = jnp.where(valid, prob_flat[picks], jnp.zeros((), prob.dtype))
        contrib, grad_weight, scaled_output, gate_gradient, up_gradient = expert_pass(input_rows, row_gradients, rows_prob, gate_weight, up_weight, down_weight)
        grad_down = group_sums(scaled_output, row_gradients, groups)
        grad_gate = group_sums(input_rows, gate_gradient, groups)
        grad_up = group_sums(input_rows, up_gradient, groups)
        contrib = lax.optimization_barrier(contrib).astype(jnp.float32)
        grad_weight = lax.optimization_barrier(grad_weight).astype(jnp.float32)
        grad_acc = grad_acc.at[rows].add(jnp.where(valid[:, None], contrib, jnp.zeros((), jnp.float32)))
        prob_acc = prob_acc.at[picks].add(jnp.where(valid, grad_weight, jnp.zeros((), jnp.float32)))
        return (grad_acc, prob_acc), (grad_gate, grad_up, grad_down)

    start_state = (jnp.zeros((TOKENS, D), jnp.float32), jnp.zeros((TOKENS * K,), jnp.float32))
    finals, stacked = lax.scan(visit, start_state, (labels, w_gate, w_up, w_down))
    grad_acc, prob_acc = finals
    grad_gate, grad_up, grad_down = stacked
    return (grad_acc.astype(jnp.bfloat16), prob_acc.reshape(TOKENS, K).astype(jnp.bfloat16), grad_gate, grad_up, grad_down)
```

```python
import jax
import jax.numpy as jnp
from jax import lax
from jax.sharding import PartitionSpec as P

F32 = jnp.float32
BF16 = jnp.bfloat16


def forward_part(input_rows, row_gradients, rows_prob, gate_weight, up_weight, down_weight):
    gate_preactivation = jnp.einsum(
        "vpc,vco->vpo", input_rows, gate_weight, preferred_element_type=jnp.float32
    )
    up_preactivation = jnp.einsum(
        "vpc,vco->vpo", input_rows, up_weight, preferred_element_type=jnp.float32
    )
    backward_rows = jnp.einsum(
        "iaj,ilj->ial", row_gradients, down_weight, preferred_element_type=jnp.float32
    )
    sigma = jax.nn.sigmoid(gate_preactivation)
    active = gate_preactivation * sigma
    hidden = active * up_preactivation
    weight_term = jnp.sum(backward_rows * hidden, axis=-1)
    weight = rows_prob.astype(jnp.float32)[..., None]
    scaled_output = (weight * hidden).astype(jnp.bfloat16)
    d_back = weight * backward_rows
    gate_gradient = (
        d_back * up_preactivation * sigma * (1.0 + gate_preactivation * (1.0 - sigma))
    ).astype(jnp.bfloat16)
    up_gradient = (d_back * active).astype(jnp.bfloat16)
    return (weight_term, scaled_output, gate_gradient, up_gradient)


def input_terms(gate_gradient, up_gradient, gate_weight, up_weight):
    leading_rows = jnp.einsum(
        "sai,sbi->sab", gate_gradient, gate_weight, preferred_element_type=jnp.float32
    )
    return leading_rows + jnp.einsum(
        "sai,sbi->sab", up_gradient, up_weight, preferred_element_type=jnp.float32
    )


def down_term(scaled_output, row_gradients):
    return jnp.einsum(
        "sub,suc->sbc", scaled_output, row_gradients, preferred_element_type=jnp.float32
    )


def gate_up_terms(input_rows, gate_gradient, up_gradient):
    gate_portion = jnp.einsum(
        "mgc,mgn->mcn", input_rows, gate_gradient, preferred_element_type=jnp.float32
    )
    up_portion = jnp.einsum(
        "mgc,mgn->mcn", input_rows, up_gradient, preferred_element_type=jnp.float32
    )
    return (gate_portion, up_portion)


def return_rows(contrib, weight_grad, select, hits):
    back_rows, back_prob = (
        lax.all_to_all(contrib, "exp", split_axis=1, concat_axis=0, tiled=True),
        lax.all_to_all(weight_grad, "exp", split_axis=1, concat_axis=0, tiled=True),
    )
    width = back_rows.shape[2]
    grad_tokens = jnp.dot(
        select, back_rows.reshape(-1, width), preferred_element_type=F32
    ).astype(BF16)
    back_prob = back_prob.reshape(-1).astype(F32)
    grad_prob = jnp.sum(jnp.where(hits, back_prob, 0.0), axis=2).astype(BF16)
    return (grad_tokens, grad_prob)


def routed_body(tokens, out_grad, route, prob, w_gate, w_up, w_down):
    local = tokens.shape[0]
    width = tokens.shape[1]
    topk = route.shape[1]
    experts = w_gate.shape[0] * lax.axis_size("exp")
    capacity = 2 * local * topk // experts
    flat = route.reshape(-1)
    labels = jnp.arange(experts, dtype=jnp.int32)
    onehot = (flat[:, None] == labels[None, :]).astype(F32)
    order = jnp.arange(local * topk, dtype=jnp.int32)
    before = (order[:, None] > order[None, :]).astype(BF16)
    earlier = jnp.dot(before, onehot.astype(BF16), preferred_element_type=F32)
    position = jnp.sum(earlier * onehot, axis=1).astype(jnp.int32)
    target = flat * capacity + position
    slots = jnp.arange(experts * capacity, dtype=jnp.int32)
    hits = target.reshape(local, topk)[:, :, None] == slots[None, None, :]
    select = jnp.sum(hits.astype(F32), axis=1).astype(BF16)
    over_rows = (((0,), (0,)), ((), ()))

    def spread(rows):
        sent = lax.dot_general(select, rows, over_rows, preferred_element_type=F32)
        return sent.astype(BF16).reshape(experts, capacity, width)

    sent_rows, sent_grad = spread(tokens), spread(out_grad)
    sent_prob = jnp.sum(jnp.where(hits, prob.astype(F32)[:, :, None], 0.0), axis=(0, 1))
    sent_prob = sent_prob.astype(BF16).reshape(experts, capacity)
    input_rows, row_gradients, rows_prob = (
        lax.all_to_all(sent_rows, "exp", split_axis=0, concat_axis=1, tiled=True),
        lax.all_to_all(sent_grad, "exp", split_axis=0, concat_axis=1, tiled=True),
        lax.all_to_all(sent_prob, "exp", split_axis=0, concat_axis=1, tiled=True),
    )
    weight_term, scaled_output, gate_gradient, up_gradient = forward_part(
        input_rows, row_gradients, rows_prob, w_gate, w_up, w_down
    )
    down_sum = down_term(scaled_output, row_gradients)
    gate_sum, up_sum = gate_up_terms(input_rows, gate_gradient, up_gradient)
    contrib = input_terms(gate_gradient, up_gradient, w_gate, w_up).astype(jnp.bfloat16)
    grad_tokens, grad_prob = return_rows(
        contrib, weight_term.astype(jnp.bfloat16), select, hits
    )
    gate_mine, up_mine, down_mine = (
        lax.psum_scatter(
            gate_sum.astype(jnp.bfloat16), "rep", scatter_dimension=1, tiled=True
        ).astype(jnp.float32),
        lax.psum_scatter(
            up_sum.astype(jnp.bfloat16), "rep", scatter_dimension=1, tiled=True
        ).astype(jnp.float32),
        lax.psum_scatter(
            down_sum.astype(jnp.bfloat16), "rep", scatter_dimension=1, tiled=True
        ).astype(jnp.float32),
    )
    grad_gate = gate_mine.astype(jnp.bfloat16)
    grad_up = up_mine.astype(jnp.bfloat16)
    grad_down = down_mine.astype(jnp.bfloat16)
    return (grad_tokens, grad_prob, grad_gate, grad_up, grad_down)


def gathered_body(tokens, out_grad, route, prob, w_gate, w_up, w_down):
    local, width = tokens.shape
    members = lax.axis_size("exp")
    experts = w_gate.shape[0] * members
    labels = jnp.arange(experts, dtype=jnp.int32)
    hit = route[:, :, None] == labels[None, None, :]
    dense = jnp.sum(jnp.where(hit, prob.astype(F32)[:, :, None], 0.0), axis=1)
    rows = lax.all_gather(tokens, "exp", axis=0, tiled=True)
    grads = lax.all_gather(out_grad, "exp", axis=0, tiled=True)
    weight = lax.all_to_all(
        dense.astype(BF16).T, "exp", split_axis=0, concat_axis=0, tiled=True
    )
    weight = weight.reshape(-1).astype(F32)[:, None]
    wg, wu, wd = w_gate[0], w_up[0], w_down[0]
    gate_pre = jnp.dot(rows, wg, preferred_element_type=F32)
    up_pre = jnp.dot(rows, wu, preferred_element_type=F32)
    back = lax.dot_general(grads, wd, (((1,), (1,)), ((), ())), preferred_element_type=F32)
    sigma = jax.nn.sigmoid(gate_pre)
    active = gate_pre * sigma
    hidden = active * up_pre
    term = jnp.sum(back * hidden, axis=-1).astype(BF16).reshape(members, local)
    scaled = (weight * hidden).astype(BF16)
    d_back = weight * back
    d_gate = (d_back * up_pre * sigma * (1.0 + gate_pre * (1.0 - sigma))).astype(BF16)
    d_up = (d_back * active).astype(BF16)
    over_last = (((1,), (1,)), ((), ()))
    contrib = lax.dot_general(d_gate, wg, over_last, preferred_element_type=F32)
    contrib = contrib + lax.dot_general(d_up, wu, over_last, preferred_element_type=F32)
    grad_tokens = lax.psum_scatter(
        contrib.astype(BF16), "exp", scatter_dimension=0, tiled=True
    )
    over_rows = (((0,), (0,)), ((), ()))
    parts = []
    for left, right in ((rows, d_gate), (rows, d_up), (scaled, grads)):
        part = lax.dot_general(left, right, over_rows, preferred_element_type=F32)
        parts.append(
            lax.psum_scatter(part.astype(BF16), "rep", scatter_dimension=0, tiled=True)[None]
        )
    term = lax.all_to_all(term, "exp", split_axis=0, concat_axis=0, tiled=True)
    picked = jnp.where(hit, term.astype(F32).T[:, None, :], 0.0)
    grad_prob = jnp.sum(picked, axis=2).astype(BF16)
    return (grad_tokens, grad_prob, *parts)


def body(tokens, out_grad, route, prob, w_gate, w_up, w_down):
    members = lax.axis_size("exp")
    experts = w_gate.shape[0] * members
    plan = gathered_body if experts <= 4 * route.shape[1] else routed_body
    return plan(tokens, out_grad, route, prob, w_gate, w_up, w_down)


def solution(mesh):
    rows = P(("rep", "exp"), None)
    held = P("exp", None, None)
    halves = P("exp", "rep", None)
    return jax.shard_map(
        body,
        mesh=mesh,
        in_specs=(rows, rows, rows, rows, held, held, held),
        out_specs=(rows, rows, halves, halves, halves),
        check_vma=False,
    )
```

```python
import jax
import jax.numpy as jnp
from jax import lax
from jax.sharding import PartitionSpec as P

F32 = jnp.float32
BF16 = jnp.bfloat16


def forward_part(input_rows, row_gradients, rows_prob, gate_weight, up_weight, down_weight):
    gate_preactivation = jnp.einsum(
        "vpc,vco->vpo", input_rows, gate_weight, preferred_element_type=jnp.float32
    )
    up_preactivation = jnp.einsum(
        "vpc,vco->vpo", input_rows, up_weight, preferred_element_type=jnp.float32
    )
    backward_rows = jnp.einsum(
        "iaj,ilj->ial", row_gradients, down_weight, preferred_element_type=jnp.float32
    )
    sigma = jax.nn.sigmoid(gate_preactivation)
    active = gate_preactivation * sigma
    hidden = active * up_preactivation
    weight_term = jnp.sum(backward_rows * hidden, axis=-1)
    weight = rows_prob.astype(jnp.float32)[..., None]
    scaled_output = (weight * hidden).astype(jnp.bfloat16)
    d_back = weight * backward_rows
    gate_gradient = (
        d_back * up_preactivation * sigma * (1.0 + gate_preactivation * (1.0 - sigma))
    ).astype(jnp.bfloat16)
    up_gradient = (d_back * active).astype(jnp.bfloat16)
    return (weight_term, scaled_output, gate_gradient, up_gradient)


def input_terms(gate_gradient, up_gradient, gate_weight, up_weight):
    leading_rows = jnp.einsum(
        "sai,sbi->sab", gate_gradient, gate_weight, preferred_element_type=jnp.float32
    )
    return leading_rows + jnp.einsum(
        "sai,sbi->sab", up_gradient, up_weight, preferred_element_type=jnp.float32
    )


def down_term(scaled_output, row_gradients):
    return jnp.einsum(
        "sub,suc->sbc", scaled_output, row_gradients, preferred_element_type=jnp.float32
    )


def gate_up_terms(input_rows, gate_gradient, up_gradient):
    gate_portion = jnp.einsum(
        "mgc,mgn->mcn", input_rows, gate_gradient, preferred_element_type=jnp.float32
    )
    up_portion = jnp.einsum(
        "mgc,mgn->mcn", input_rows, up_gradient, preferred_element_type=jnp.float32
    )
    return (gate_portion, up_portion)


def return_rows(contrib, weight_grad, select, hits):
    back_rows, back_prob = (
        lax.all_to_all(contrib, "exp", split_axis=1, concat_axis=0, tiled=True),
        lax.all_to_all(weight_grad, "exp", split_axis=1, concat_axis=0, tiled=True),
    )
    width = back_rows.shape[2]
    grad_tokens = jnp.dot(
        select, back_rows.reshape(-1, width), preferred_element_type=F32
    ).astype(BF16)
    back_prob = back_prob.reshape(-1).astype(F32)
    grad_prob = jnp.sum(jnp.where(hits, back_prob, 0.0), axis=2).astype(BF16)
    return (grad_tokens, grad_prob)


def routed_body(tokens, out_grad, route, prob, w_gate, w_up, w_down):
    local = tokens.shape[0]
    width = tokens.shape[1]
    topk = route.shape[1]
    experts = w_gate.shape[0] * lax.axis_size("exp")
    capacity = 2 * local * topk // experts
    flat = route.reshape(-1)
    labels = jnp.arange(experts, dtype=jnp.int32)
    onehot = (flat[:, None] == labels[None, :]).astype(F32)
    order = jnp.arange(local * topk, dtype=jnp.int32)
    before = (order[:, None] > order[None, :]).astype(BF16)
    earlier = jnp.dot(before, onehot.astype(BF16), preferred_element_type=F32)
    position = jnp.sum(earlier * onehot, axis=1).astype(jnp.int32)
    target = flat * capacity + position
    slots = jnp.arange(experts * capacity, dtype=jnp.int32)
    hits = target.reshape(local, topk)[:, :, None] == slots[None, None, :]
    select = jnp.sum(hits.astype(F32), axis=1).astype(BF16)
    over_rows = (((0,), (0,)), ((), ()))

    def spread(rows):
        sent = lax.dot_general(select, rows, over_rows, preferred_element_type=F32)
        return sent.astype(BF16).reshape(experts, capacity, width)

    sent_rows, sent_grad = spread(tokens), spread(out_grad)
    sent_prob = jnp.sum(jnp.where(hits, prob.astype(F32)[:, :, None], 0.0), axis=(0, 1))
    sent_prob = sent_prob.astype(BF16).reshape(experts, capacity)
    input_rows, row_gradients, rows_prob = (
        lax.all_to_all(sent_rows, "exp", split_axis=0, concat_axis=1, tiled=True),
        lax.all_to_all(sent_grad, "exp", split_axis=0, concat_axis=1, tiled=True),
        lax.all_to_all(sent_prob, "exp", split_axis=0, concat_axis=1, tiled=True),
    )
    weight_term, scaled_output, gate_gradient, up_gradient = forward_part(
        input_rows, row_gradients, rows_prob, w_gate, w_up, w_down
    )
    down_sum = down_term(scaled_output, row_gradients)
    gate_sum, up_sum = gate_up_terms(input_rows, gate_gradient, up_gradient)
    contrib = input_terms(gate_gradient, up_gradient, w_gate, w_up).astype(jnp.bfloat16)
    grad_tokens, grad_prob = return_rows(
        contrib, weight_term.astype(jnp.bfloat16), select, hits
    )
    gate_mine, up_mine, down_mine = (
        lax.psum_scatter(
            gate_sum.astype(jnp.bfloat16), "rep", scatter_dimension=1, tiled=True
        ).astype(jnp.float32),
        lax.psum_scatter(
            up_sum.astype(jnp.bfloat16), "rep", scatter_dimension=1, tiled=True
        ).astype(jnp.float32),
        lax.psum_scatter(
            down_sum.astype(jnp.bfloat16), "rep", scatter_dimension=1, tiled=True
        ).astype(jnp.float32),
    )
    grad_gate = gate_mine.astype(jnp.bfloat16)
    grad_up = up_mine.astype(jnp.bfloat16)
    grad_down = down_mine.astype(jnp.bfloat16)
    return (grad_tokens, grad_prob, grad_gate, grad_up, grad_down)


def across(part, axis):
    if lax.axis_size(axis) != 2:
        return lax.psum_scatter(part, axis, scatter_dimension=0, tiled=True)
    half = part.shape[0] // 2
    me = lax.axis_index(axis)
    theirs = lax.dynamic_slice_in_dim(part, (1 - me) * half, half, 0)
    mine = lax.dynamic_slice_in_dim(part, me * half, half, 0)
    arrived = lax.ppermute(theirs, axis, [(0, 1), (1, 0)])
    return (mine.astype(F32) + arrived.astype(F32)).astype(BF16)


def gathered_body(tokens, out_grad, route, prob, w_gate, w_up, w_down):
    local, width = tokens.shape
    members = lax.axis_size("exp")
    chips = members // 2
    experts = w_gate.shape[0] * members
    core = lax.rem(lax.axis_index("exp"), 2)
    alike = [[2 * chip + c for chip in range(chips)] for c in range(2)]
    swap = [(i, i ^ 1) for i in range(members)]
    labels = jnp.arange(experts, dtype=jnp.int32)
    hit = route[:, :, None] == labels[None, None, :]
    dense = jnp.sum(jnp.where(hit, prob.astype(F32)[:, :, None], 0.0), axis=1)
    weight = lax.all_to_all(
        dense.astype(BF16).T, "exp", split_axis=0, concat_axis=0, tiled=True
    ).reshape(chips, 2, local)

    def gather(rows):
        own = lax.all_gather(rows, "exp", axis_index_groups=alike, axis=0, tiled=True)
        return own, lax.ppermute(own, "exp", swap)

    rows = gather(tokens)
    grads = gather(out_grad)
    wg, wu, wd = w_gate[0], w_up[0], w_down[0]
    over_last = (((1,), (1,)), ((), ()))
    over_rows = (((0,), (0,)), ((), ()))

    def forward(side):
        place = core if side == 0 else 1 - core
        prob_rows = lax.dynamic_index_in_dim(weight, place, 1, keepdims=False)
        prob_rows = prob_rows.reshape(-1).astype(F32)[:, None]
        gate_pre = jnp.dot(rows[side], wg, preferred_element_type=F32)
        up_pre = jnp.dot(rows[side], wu, preferred_element_type=F32)
        back = lax.dot_general(grads[side], wd, over_last, preferred_element_type=F32)
        sigma = jax.nn.sigmoid(gate_pre)
        active = gate_pre * sigma
        hidden = active * up_pre
        term = jnp.sum(back * hidden, axis=-1).astype(BF16).reshape(chips, local)
        scaled = (prob_rows * hidden).astype(BF16)
        d_back = prob_rows * back
        slope = sigma * (1.0 + gate_pre * (1.0 - sigma))
        d_gate = (d_back * up_pre * slope).astype(BF16)
        d_up = (d_back * active).astype(BF16)
        contrib = lax.dot_general(d_gate, wg, over_last, preferred_element_type=F32)
        contrib += lax.dot_general(d_up, wu, over_last, preferred_element_type=F32)
        return term, scaled, d_gate, d_up, contrib

    far = forward(1)
    arrived = lax.ppermute(far[4].astype(BF16), "exp", swap)
    near = forward(0)
    summed = (near[4] + arrived.astype(F32)).astype(BF16)
    grad_tokens = lax.psum_scatter(
        summed, "exp", scatter_dimension=0, axis_index_groups=alike, tiled=True
    )

    def outer(left, right):
        total = sum(
            lax.dot_general(a, b, over_rows, preferred_element_type=F32)
            for a, b in zip(left, right)
        )
        return across(total.astype(BF16), "rep")[None]

    scaled, d_gate, d_up = ((near[n], far[n]) for n in (1, 2, 3))
    grad_gate = outer(rows, d_gate)
    grad_up = outer(rows, d_up)
    grad_down = outer(scaled, grads)
    flip = core == 1
    first = jnp.where(flip, far[0], near[0])
    second = jnp.where(flip, near[0], far[0])
    term = jnp.stack((first, second), axis=1).reshape(members, local)
    term = lax.all_to_all(term, "exp", split_axis=0, concat_axis=0, tiled=True)
    picked = jnp.where(hit, term.astype(F32).T[:, None, :], 0.0)
    grad_prob = jnp.sum(picked, axis=2).astype(BF16)
    return (grad_tokens, grad_prob, grad_gate, grad_up, grad_down)


def body(tokens, out_grad, route, prob, w_gate, w_up, w_down):
    members = lax.axis_size("exp")
    experts = w_gate.shape[0] * members
    plan = gathered_body if experts <= 4 * route.shape[1] else routed_body
    return plan(tokens, out_grad, route, prob, w_gate, w_up, w_down)


def solution(mesh):
    rows = P(("rep", "exp"), None)
    held = P("exp", None, None)
    halves = P("exp", "rep", None)
    return jax.shard_map(
        body,
        mesh=mesh,
        in_specs=(rows, rows, rows, rows, held, held, held),
        out_specs=(rows, rows, halves, halves, halves),
        check_vma=False,
    )
```

```python
import jax
import jax.numpy as jnp
from jax import lax
from jax.sharding import PartitionSpec as P

F32 = jnp.float32
BF16 = jnp.bfloat16


def forward_part(input_rows, row_gradients, rows_prob, gate_weight, up_weight, down_weight):
    gate_preactivation = jnp.einsum(
        "vpc,vco->vpo", input_rows, gate_weight, preferred_element_type=jnp.float32
    )
    up_preactivation = jnp.einsum(
        "vpc,vco->vpo", input_rows, up_weight, preferred_element_type=jnp.float32
    )
    backward_rows = jnp.einsum(
        "iaj,ilj->ial", row_gradients, down_weight, preferred_element_type=jnp.float32
    )
    sigma = jax.nn.sigmoid(gate_preactivation)
    active = gate_preactivation * sigma
    hidden = active * up_preactivation
    weight_term = jnp.sum(backward_rows * hidden, axis=-1)
    weight = rows_prob.astype(jnp.float32)[..., None]
    scaled_output = (weight * hidden).astype(jnp.bfloat16)
    d_back = weight * backward_rows
    gate_gradient = (
        d_back * up_preactivation * sigma * (1.0 + gate_preactivation * (1.0 - sigma))
    ).astype(jnp.bfloat16)
    up_gradient = (d_back * active).astype(jnp.bfloat16)
    return (weight_term, scaled_output, gate_gradient, up_gradient)


def input_terms(gate_gradient, up_gradient, gate_weight, up_weight):
    leading_rows = jnp.einsum(
        "sai,sbi->sab", gate_gradient, gate_weight, preferred_element_type=jnp.float32
    )
    return leading_rows + jnp.einsum(
        "sai,sbi->sab", up_gradient, up_weight, preferred_element_type=jnp.float32
    )


def down_term(scaled_output, row_gradients):
    return jnp.einsum(
        "sub,suc->sbc", scaled_output, row_gradients, preferred_element_type=jnp.float32
    )


def gate_up_terms(input_rows, gate_gradient, up_gradient):
    gate_portion = jnp.einsum(
        "mgc,mgn->mcn", input_rows, gate_gradient, preferred_element_type=jnp.float32
    )
    up_portion = jnp.einsum(
        "mgc,mgn->mcn", input_rows, up_gradient, preferred_element_type=jnp.float32
    )
    return (gate_portion, up_portion)


def return_rows(contrib, weight_grad, select, hits):
    back_rows, back_prob = (
        lax.all_to_all(contrib, "exp", split_axis=1, concat_axis=0, tiled=True),
        lax.all_to_all(weight_grad, "exp", split_axis=1, concat_axis=0, tiled=True),
    )
    width = back_rows.shape[2]
    grad_tokens = jnp.dot(
        select, back_rows.reshape(-1, width), preferred_element_type=F32
    ).astype(BF16)
    back_prob = back_prob.reshape(-1).astype(F32)
    grad_prob = jnp.sum(jnp.where(hits, back_prob, 0.0), axis=2).astype(BF16)
    return (grad_tokens, grad_prob)


def routed_body(tokens, out_grad, route, prob, w_gate, w_up, w_down):
    local = tokens.shape[0]
    width = tokens.shape[1]
    topk = route.shape[1]
    experts = w_gate.shape[0] * lax.axis_size("exp")
    capacity = 2 * local * topk // experts
    flat = route.reshape(-1)
    labels = jnp.arange(experts, dtype=jnp.int32)
    onehot = (flat[:, None] == labels[None, :]).astype(F32)
    order = jnp.arange(local * topk, dtype=jnp.int32)
    before = (order[:, None] > order[None, :]).astype(BF16)
    earlier = jnp.dot(before, onehot.astype(BF16), preferred_element_type=F32)
    position = jnp.sum(earlier * onehot, axis=1).astype(jnp.int32)
    target = flat * capacity + position
    slots = jnp.arange(experts * capacity, dtype=jnp.int32)
    hits = target.reshape(local, topk)[:, :, None] == slots[None, None, :]
    select = jnp.sum(hits.astype(F32), axis=1).astype(BF16)
    over_rows = (((0,), (0,)), ((), ()))

    def spread(rows):
        sent = lax.dot_general(select, rows, over_rows, preferred_element_type=F32)
        return sent.astype(BF16).reshape(experts, capacity, width)

    sent_rows, sent_grad = spread(tokens), spread(out_grad)
    sent_prob = jnp.sum(jnp.where(hits, prob.astype(F32)[:, :, None], 0.0), axis=(0, 1))
    sent_prob = sent_prob.astype(BF16).reshape(experts, capacity)
    input_rows, row_gradients, rows_prob = (
        lax.all_to_all(sent_rows, "exp", split_axis=0, concat_axis=1, tiled=True),
        lax.all_to_all(sent_grad, "exp", split_axis=0, concat_axis=1, tiled=True),
        lax.all_to_all(sent_prob, "exp", split_axis=0, concat_axis=1, tiled=True),
    )
    weight_term, scaled_output, gate_gradient, up_gradient = forward_part(
        input_rows, row_gradients, rows_prob, w_gate, w_up, w_down
    )
    down_sum = down_term(scaled_output, row_gradients)
    gate_sum, up_sum = gate_up_terms(input_rows, gate_gradient, up_gradient)
    contrib = input_terms(gate_gradient, up_gradient, w_gate, w_up).astype(jnp.bfloat16)
    grad_tokens, grad_prob = return_rows(
        contrib, weight_term.astype(jnp.bfloat16), select, hits
    )
    gate_mine, up_mine, down_mine = (
        lax.psum_scatter(
            gate_sum.astype(jnp.bfloat16), "rep", scatter_dimension=1, tiled=True
        ).astype(jnp.float32),
        lax.psum_scatter(
            up_sum.astype(jnp.bfloat16), "rep", scatter_dimension=1, tiled=True
        ).astype(jnp.float32),
        lax.psum_scatter(
            down_sum.astype(jnp.bfloat16), "rep", scatter_dimension=1, tiled=True
        ).astype(jnp.float32),
    )
    grad_gate = gate_mine.astype(jnp.bfloat16)
    grad_up = up_mine.astype(jnp.bfloat16)
    grad_down = down_mine.astype(jnp.bfloat16)
    return (grad_tokens, grad_prob, grad_gate, grad_up, grad_down)


def across(part, axis):
    if lax.axis_size(axis) != 2:
        return lax.psum_scatter(part, axis, scatter_dimension=0, tiled=True)
    half = part.shape[0] // 2
    me = lax.axis_index(axis)
    theirs = lax.dynamic_slice_in_dim(part, (1 - me) * half, half, 0)
    mine = lax.dynamic_slice_in_dim(part, me * half, half, 0)
    arrived = lax.ppermute(theirs, axis, [(0, 1), (1, 0)])
    return (mine.astype(F32) + arrived.astype(F32)).astype(BF16)


def gathered_body(tokens, out_grad, route, prob, w_gate, w_up, w_down):
    local, width = tokens.shape
    members = lax.axis_size("exp")
    chips = members // 2
    experts = w_gate.shape[0] * members
    core = lax.rem(lax.axis_index("exp"), 2)
    chip = lax.axis_index("exp") // 2
    ring = list(range(0, chips, 2)) + list(range(1, chips, 2))[::-1]
    half = chips // 2
    spot = jnp.where(chip % 2 == 0, chip // 2, chips - 1 - chip // 2)
    ahead, behind = (
        [
            (2 * ring[p] + c, 2 * ring[(p + step) % chips] + c)
            for p in range(chips)
            for c in range(2)
        ]
        for step in (1, -1)
    )
    offsets = [0] + [sign * step for step in range(1, half) for sign in (-1, 1)] + [half]
    middle = width // 2
    swap = [(i, i ^ 1) for i in range(members)]
    sources = jnp.remainder(spot + jnp.array(offsets, jnp.int32), chips)
    sources = jnp.where(sources < half, 2 * sources, 2 * (chips - 1 - sources) + 1)

    def chosen(place):
        ids = jnp.arange(members, dtype=jnp.int32)
        return (2 * sources[:, None] + place == ids[None, :]).astype(BF16)

    near_pick, far_pick = chosen(core), chosen(1 - core)
    labels = jnp.arange(experts, dtype=jnp.int32)
    hit = route[:, :, None] == labels[None, None, :]
    dense = jnp.sum(jnp.where(hit, prob.astype(F32)[:, :, None], 0.0), axis=1)
    weight = lax.all_to_all(
        dense.astype(BF16).T, "exp", split_axis=0, concat_axis=0, tiled=True
    ).reshape(members, local)

    def gather(rows):
        blocks = [rows]
        right = left = rows
        for _ in range(1, half):
            right = lax.ppermute(right, "exp", ahead)
            left = lax.ppermute(left, "exp", behind)
            blocks += [right, left]
        blocks.append(
            jnp.concatenate(
                (
                    lax.ppermute(right[:, :middle], "exp", ahead),
                    lax.ppermute(left[:, middle:], "exp", behind),
                ),
                axis=1,
            )
        )
        own = jnp.concatenate(blocks, axis=0)
        return own, lax.ppermute(own, "exp", swap)

    def give_back(terms):
        def term(offset):
            at = offsets.index(offset) * local
            return terms[at : at + local]

        def add(held, arrived):
            return (held.astype(F32) + arrived.astype(F32)).astype(BF16)

        right = lax.ppermute(term(half)[:, :middle], "exp", ahead)
        left = lax.ppermute(term(half)[:, middle:], "exp", behind)
        for step in range(half - 1, 0, -1):
            held, other = term(step), term(-step)
            if step == half - 1:
                right = jnp.concatenate((add(held[:, :middle], right), held[:, middle:]), axis=1)
                left = jnp.concatenate((other[:, :middle], add(other[:, middle:], left)), axis=1)
            else:
                right, left = add(held, right), add(other, left)
            right = lax.ppermute(right, "exp", ahead)
            left = lax.ppermute(left, "exp", behind)
        total = term(0).astype(F32) + right.astype(F32) + left.astype(F32)
        return total.astype(BF16)

    rows = gather(tokens)
    grads = gather(out_grad)
    wg, wu, wd = w_gate[0], w_up[0], w_down[0]
    over_last = (((1,), (1,)), ((), ()))
    over_rows = (((0,), (0,)), ((), ()))

    def forward(side):
        pick = near_pick if side == 0 else far_pick
        prob_rows = jnp.dot(pick, weight, preferred_element_type=F32).reshape(-1)[:, None]
        gate_pre = jnp.dot(rows[side], wg, preferred_element_type=F32)
        up_pre = jnp.dot(rows[side], wu, preferred_element_type=F32)
        back = lax.dot_general(grads[side], wd, over_last, preferred_element_type=F32)
        sigma = jax.nn.sigmoid(gate_pre)
        active = gate_pre * sigma
        hidden = active * up_pre
        term = jnp.sum(back * hidden, axis=-1).astype(BF16).reshape(chips, local)
        scaled = (prob_rows * hidden).astype(BF16)
        d_back = prob_rows * back
        slope = sigma * (1.0 + gate_pre * (1.0 - sigma))
        d_gate = (d_back * up_pre * slope).astype(BF16)
        d_up = (d_back * active).astype(BF16)
        contrib = lax.dot_general(d_gate, wg, over_last, preferred_element_type=F32)
        contrib += lax.dot_general(d_up, wu, over_last, preferred_element_type=F32)
        return term, scaled, d_gate, d_up, contrib

    far = forward(1)
    arrived = lax.ppermute(far[4].astype(BF16), "exp", swap)
    near = forward(0)
    summed = (near[4] + arrived.astype(F32)).astype(BF16)
    grad_tokens = give_back(summed)

    def outer(left, right):
        total = sum(
            lax.dot_general(a, b, over_rows, preferred_element_type=F32)
            for a, b in zip(left, right)
        )
        return across(total.astype(BF16), "rep")[None]

    scaled, d_gate, d_up = ((near[n], far[n]) for n in (1, 2, 3))
    grad_gate = outer(rows, d_gate)
    grad_up = outer(rows, d_up)
    grad_down = outer(scaled, grads)
    term = lax.dot_general(near_pick, near[0], over_rows, preferred_element_type=F32)
    term += lax.dot_general(far_pick, far[0], over_rows, preferred_element_type=F32)
    term = term.astype(BF16)
    term = lax.all_to_all(term, "exp", split_axis=0, concat_axis=0, tiled=True)
    picked = jnp.where(hit, term.astype(F32).T[:, None, :], 0.0)
    grad_prob = jnp.sum(picked, axis=2).astype(BF16)
    return (grad_tokens, grad_prob, grad_gate, grad_up, grad_down)


def body(tokens, out_grad, route, prob, w_gate, w_up, w_down):
    members = lax.axis_size("exp")
    experts = w_gate.shape[0] * members
    near = experts <= 4 * route.shape[1] and members >= 8 and members % 4 == 0
    plan = gathered_body if near else routed_body
    return plan(tokens, out_grad, route, prob, w_gate, w_up, w_down)


def solution(mesh):
    rows = P(("rep", "exp"), None)
    held = P("exp", None, None)
    halves = P("exp", "rep", None)
    return jax.shard_map(
        body,
        mesh=mesh,
        in_specs=(rows, rows, rows, rows, held, held, held),
        out_specs=(rows, rows, halves, halves, halves),
        check_vma=False,
    )
```

```python
import jax
import jax.numpy as jnp
from jax import lax
from jax.sharding import PartitionSpec as P

F32 = jnp.float32
BF16 = jnp.bfloat16


def forward_part(input_rows, row_gradients, rows_prob, gate_weight, up_weight, down_weight):
    gate_preactivation = jnp.einsum(
        "vpc,vco->vpo", input_rows, gate_weight, preferred_element_type=jnp.float32
    )
    up_preactivation = jnp.einsum(
        "vpc,vco->vpo", input_rows, up_weight, preferred_element_type=jnp.float32
    )
    backward_rows = jnp.einsum(
        "iaj,ilj->ial", row_gradients, down_weight, preferred_element_type=jnp.float32
    )
    sigma = jax.nn.sigmoid(gate_preactivation)
    active = gate_preactivation * sigma
    hidden = active * up_preactivation
    weight_term = jnp.sum(backward_rows * hidden, axis=-1)
    weight = rows_prob.astype(jnp.float32)[..., None]
    scaled_output = (weight * hidden).astype(jnp.bfloat16)
    d_back = weight * backward_rows
    gate_gradient = (
        d_back * up_preactivation * sigma * (1.0 + gate_preactivation * (1.0 - sigma))
    ).astype(jnp.bfloat16)
    up_gradient = (d_back * active).astype(jnp.bfloat16)
    return (weight_term, scaled_output, gate_gradient, up_gradient)


def input_terms(gate_gradient, up_gradient, gate_weight, up_weight):
    leading_rows = jnp.einsum(
        "sai,sbi->sab", gate_gradient, gate_weight, preferred_element_type=jnp.float32
    )
    return leading_rows + jnp.einsum(
        "sai,sbi->sab", up_gradient, up_weight, preferred_element_type=jnp.float32
    )


def down_term(scaled_output, row_gradients):
    return jnp.einsum(
        "sub,suc->sbc", scaled_output, row_gradients, preferred_element_type=jnp.float32
    )


def gate_up_terms(input_rows, gate_gradient, up_gradient):
    gate_portion = jnp.einsum(
        "mgc,mgn->mcn", input_rows, gate_gradient, preferred_element_type=jnp.float32
    )
    up_portion = jnp.einsum(
        "mgc,mgn->mcn", input_rows, up_gradient, preferred_element_type=jnp.float32
    )
    return (gate_portion, up_portion)


def return_rows(contrib, weight_grad, select, hits):
    back_rows, back_prob = (
        lax.all_to_all(contrib, "exp", split_axis=1, concat_axis=0, tiled=True),
        lax.all_to_all(weight_grad, "exp", split_axis=1, concat_axis=0, tiled=True),
    )
    width = back_rows.shape[2]
    grad_tokens = jnp.dot(
        select, back_rows.reshape(-1, width), preferred_element_type=F32
    ).astype(BF16)
    back_prob = back_prob.reshape(-1).astype(F32)
    grad_prob = jnp.sum(jnp.where(hits, back_prob, 0.0), axis=2).astype(BF16)
    return (grad_tokens, grad_prob)


def routed_body(tokens, out_grad, route, prob, w_gate, w_up, w_down):
    local = tokens.shape[0]
    width = tokens.shape[1]
    topk = route.shape[1]
    experts = w_gate.shape[0] * lax.axis_size("exp")
    capacity = 2 * local * topk // experts
    flat = route.reshape(-1)
    labels = jnp.arange(experts, dtype=jnp.int32)
    onehot = (flat[:, None] == labels[None, :]).astype(F32)
    order = jnp.arange(local * topk, dtype=jnp.int32)
    before = (order[:, None] > order[None, :]).astype(BF16)
    earlier = jnp.dot(before, onehot.astype(BF16), preferred_element_type=F32)
    position = jnp.sum(earlier * onehot, axis=1).astype(jnp.int32)
    target = flat * capacity + position
    slots = jnp.arange(experts * capacity, dtype=jnp.int32)
    hits = target.reshape(local, topk)[:, :, None] == slots[None, None, :]
    select = jnp.sum(hits.astype(F32), axis=1).astype(BF16)
    over_rows = (((0,), (0,)), ((), ()))

    def spread(rows):
        sent = lax.dot_general(select, rows, over_rows, preferred_element_type=F32)
        return sent.astype(BF16).reshape(experts, capacity, width)

    sent_rows, sent_grad = spread(tokens), spread(out_grad)
    sent_prob = jnp.sum(jnp.where(hits, prob.astype(F32)[:, :, None], 0.0), axis=(0, 1))
    sent_prob = sent_prob.astype(BF16).reshape(experts, capacity)
    input_rows, row_gradients, rows_prob = (
        lax.all_to_all(sent_rows, "exp", split_axis=0, concat_axis=1, tiled=True),
        lax.all_to_all(sent_grad, "exp", split_axis=0, concat_axis=1, tiled=True),
        lax.all_to_all(sent_prob, "exp", split_axis=0, concat_axis=1, tiled=True),
    )
    weight_term, scaled_output, gate_gradient, up_gradient = forward_part(
        input_rows, row_gradients, rows_prob, w_gate, w_up, w_down
    )
    down_sum = down_term(scaled_output, row_gradients)
    gate_sum, up_sum = gate_up_terms(input_rows, gate_gradient, up_gradient)
    contrib = input_terms(gate_gradient, up_gradient, w_gate, w_up).astype(jnp.bfloat16)
    grad_tokens, grad_prob = return_rows(
        contrib, weight_term.astype(jnp.bfloat16), select, hits
    )
    gate_mine, up_mine, down_mine = (
        lax.psum_scatter(
            gate_sum.astype(jnp.bfloat16), "rep", scatter_dimension=1, tiled=True
        ).astype(jnp.float32),
        lax.psum_scatter(
            up_sum.astype(jnp.bfloat16), "rep", scatter_dimension=1, tiled=True
        ).astype(jnp.float32),
        lax.psum_scatter(
            down_sum.astype(jnp.bfloat16), "rep", scatter_dimension=1, tiled=True
        ).astype(jnp.float32),
    )
    grad_gate = gate_mine.astype(jnp.bfloat16)
    grad_up = up_mine.astype(jnp.bfloat16)
    grad_down = down_mine.astype(jnp.bfloat16)
    return (grad_tokens, grad_prob, grad_gate, grad_up, grad_down)


def across(part, axis):
    if lax.axis_size(axis) != 2:
        return lax.psum_scatter(part, axis, scatter_dimension=0, tiled=True)
    half = part.shape[0] // 2
    me = lax.axis_index(axis)
    theirs = lax.dynamic_slice_in_dim(part, (1 - me) * half, half, 0)
    mine = lax.dynamic_slice_in_dim(part, me * half, half, 0)
    arrived = lax.ppermute(theirs, axis, [(0, 1), (1, 0)])
    return (mine.astype(F32) + arrived.astype(F32)).astype(BF16)


def gathered_body(tokens, out_grad, route, prob, w_gate, w_up, w_down):
    local, width = tokens.shape
    members = lax.axis_size("exp")
    chips = members // 2
    experts = w_gate.shape[0] * members
    core = lax.rem(lax.axis_index("exp"), 2)
    chip = lax.axis_index("exp") // 2
    ring = list(range(0, chips, 2)) + list(range(1, chips, 2))[::-1]
    half = chips // 2
    spot = jnp.where(chip % 2 == 0, chip // 2, chips - 1 - chip // 2)
    ahead, behind = (
        [
            (2 * ring[p] + c, 2 * ring[(p + step) % chips] + c)
            for p in range(chips)
            for c in range(2)
        ]
        for step in (1, -1)
    )
    offsets = [0] + [sign * step for step in range(1, half) for sign in (-1, 1)] + [half]
    middle = width // 2
    swap = [(i, i ^ 1) for i in range(members)]
    sources = jnp.remainder(spot + jnp.array(offsets, jnp.int32), chips)
    sources = jnp.where(sources < half, 2 * sources, 2 * (chips - 1 - sources) + 1)

    def chosen(place):
        ids = jnp.arange(members, dtype=jnp.int32)
        return (2 * sources[:, None] + place == ids[None, :]).astype(BF16)

    near_pick, far_pick = chosen(core), chosen(1 - core)
    labels = jnp.arange(experts, dtype=jnp.int32)
    hit = route[:, :, None] == labels[None, None, :]
    dense = jnp.sum(jnp.where(hit, prob.astype(F32)[:, :, None], 0.0), axis=1)
    weight = lax.all_to_all(
        dense.astype(BF16).T, "exp", split_axis=0, concat_axis=0, tiled=True
    ).reshape(members, local)

    def gather(rows, beside):
        blocks = [rows]
        right = left = rows
        for step in range(1, half):
            right = lax.ppermute(right, "exp", ahead)
            left = lax.ppermute(left, "exp", behind)
            if step == 1:
                right, beside = lax.optimization_barrier((right, beside))
            blocks += [right, left]
        blocks.append(
            jnp.concatenate(
                (
                    lax.ppermute(right[:, :middle], "exp", ahead),
                    lax.ppermute(left[:, middle:], "exp", behind),
                ),
                axis=1,
            )
        )
        own = jnp.concatenate(blocks, axis=0)
        return (own, lax.ppermute(own, "exp", swap)), beside

    def give_back(terms):
        def term(offset):
            at = offsets.index(offset) * local
            return terms[at : at + local]

        def add(held, arrived):
            return (held.astype(F32) + arrived.astype(F32)).astype(BF16)

        right = lax.ppermute(term(half)[:, :middle], "exp", ahead)
        left = lax.ppermute(term(half)[:, middle:], "exp", behind)
        for step in range(half - 1, 0, -1):
            held, other = term(step), term(-step)
            if step == half - 1:
                right = jnp.concatenate((add(held[:, :middle], right), held[:, middle:]), axis=1)
                left = jnp.concatenate((other[:, :middle], add(other[:, middle:], left)), axis=1)
            else:
                right, left = add(held, right), add(other, left)
            right = lax.ppermute(right, "exp", ahead)
            left = lax.ppermute(left, "exp", behind)
        total = term(0).astype(F32) + right.astype(F32) + left.astype(F32)
        return total.astype(BF16)

    rows, weight = gather(tokens, weight)
    grads, weight = gather(out_grad, weight)
    wg, wu, wd = w_gate[0], w_up[0], w_down[0]
    over_last = (((1,), (1,)), ((), ()))
    over_rows = (((0,), (0,)), ((), ()))

    def forward(side):
        pick = near_pick if side == 0 else far_pick
        prob_rows = jnp.dot(pick, weight, preferred_element_type=F32).reshape(-1)[:, None]
        gate_pre = jnp.dot(rows[side], wg, preferred_element_type=F32)
        up_pre = jnp.dot(rows[side], wu, preferred_element_type=F32)
        back = lax.dot_general(grads[side], wd, over_last, preferred_element_type=F32)
        sigma = jax.nn.sigmoid(gate_pre)
        active = gate_pre * sigma
        hidden = active * up_pre
        term = jnp.sum(back * hidden, axis=-1).astype(BF16).reshape(chips, local)
        scaled = (prob_rows * hidden).astype(BF16)
        d_back = prob_rows * back
        slope = sigma * (1.0 + gate_pre * (1.0 - sigma))
        d_gate = (d_back * up_pre * slope).astype(BF16)
        d_up = (d_back * active).astype(BF16)
        contrib = lax.dot_general(d_gate, wg, over_last, preferred_element_type=F32)
        contrib += lax.dot_general(d_up, wu, over_last, preferred_element_type=F32)
        return term, scaled, d_gate, d_up, contrib

    far = forward(1)
    arrived = lax.ppermute(far[4].astype(BF16), "exp", swap)
    near = forward(0)
    summed = (near[4] + arrived.astype(F32)).astype(BF16)
    grad_tokens = give_back(summed)

    def outer(left, right):
        total = sum(
            lax.dot_general(a, b, over_rows, preferred_element_type=F32)
            for a, b in zip(left, right)
        )
        return total.astype(BF16)

    scaled, d_gate, d_up = ((near[n], far[n]) for n in (1, 2, 3))
    gate_total = outer(rows, d_gate)
    up_total = outer(rows, d_up)
    down_total = outer(scaled, grads)
    grad_gate = across(gate_total, "rep")[None]
    grad_up = across(up_total, "rep")[None]
    term = lax.dot_general(near_pick, near[0], over_rows, preferred_element_type=F32)
    term += lax.dot_general(far_pick, far[0], over_rows, preferred_element_type=F32)
    term, down_total = lax.optimization_barrier((term.astype(BF16), down_total))
    grad_down = across(down_total, "rep")[None]
    term = lax.all_to_all(term, "exp", split_axis=0, concat_axis=0, tiled=True)
    picked = jnp.where(hit, term.astype(F32).T[:, None, :], 0.0)
    grad_prob = jnp.sum(picked, axis=2).astype(BF16)
    return (grad_tokens, grad_prob, grad_gate, grad_up, grad_down)


def body(tokens, out_grad, route, prob, w_gate, w_up, w_down):
    members = lax.axis_size("exp")
    experts = w_gate.shape[0] * members
    near = experts <= 4 * route.shape[1] and members >= 8 and members % 4 == 0
    plan = gathered_body if near else routed_body
    return plan(tokens, out_grad, route, prob, w_gate, w_up, w_down)


def solution(mesh):
    rows = P(("rep", "exp"), None)
    held = P("exp", None, None)
    halves = P("exp", "rep", None)
    return jax.shard_map(
        body,
        mesh=mesh,
        in_specs=(rows, rows, rows, rows, held, held, held),
        out_specs=(rows, rows, halves, halves, halves),
        check_vma=False,
    )
```
